256 devices in a mesh: dp: 64 (over z, y, x_hi), pipe: 2 (over core), tensor: 2 (over x_lo).
Axes of the slice: x: 4 (x_hi: 2, x_lo: 2; x = x_hi * 2 + x_lo), y: 4, z: 8, core: 2. Of those that a mesh axis runs over, the one named last changes fastest.
Arguments:
- activations: bfloat16 [2, 32768, 4096], P('pipe', ('dp', 'tensor')), may hold values from -6 to 6
- norm_gain: float32 [2, 4096], P('pipe'), may hold values from 0.5 to 1.5
- value_weight: bfloat16 [2, 4096, 512], P('pipe', None, 'tensor'), may hold values from -0.75 to 0.75
- upstream_grad: bfloat16 [2, 32768, 512], P('pipe', 'dp', 'tensor'), may hold values from -4 to 4
- error_buffer: bfloat16 [2, 262144, 512], P('pipe', 'dp', 'tensor'), may hold values from -12 to 12
- prior_basis: float32 [2, 512, 32], P('pipe', 'tensor'), may hold values from -6 to 6
Outputs:
- received_grad: bfloat16 [2, 32768, 4096], P('pipe', ('dp', 'tensor'))
- left_factor: float32 [2, 8192, 32], P('pipe', 'tensor')
- right_factor: float32 [2, 512, 32], P('pipe', 'tensor')
- error_next: bfloat16 [2, 262144, 512], P('pipe', 'dp', 'tensor')
The draws below stay inside these ranges and needn't reach their ends.
All inputs are finite; a program needn't handle non-finite values.
Results may differ from the reference program's by a relative error of at most 0.0049.
Values may be sent and summed in bfloat16 or wider, within the bound.
No kernel may reach another device: no remote copies, remote signals or barrier semaphores. Data moves between devices by JAX's collectives and lax.ppermute only.
A program may use at most 64 MiB of HBM per device.

```python
import math
import jax
import jax.numpy as jnp
from jax import lax

D = 4096
RANK = 32
TOK_DEV = 512
V_DEV = 256
VW = 512
TOKENS = 32768
SECTIONS = 2
ERR_ROWS = 262144
N_DP = 64
N_TENSOR = 2


def draw_upstream_grad(key, part):
    key = jax.random.fold_in(key, 7)
    key_base, key_rows = jax.random.split(key, 2)
    section_rise = 1.0 + 2.0 * jnp.arange(SECTIONS, dtype=jnp.float32) / max(SECTIONS - 1, 1)
    column_rise = 1.0 + jnp.arange(VW, dtype=jnp.float32) / max(VW - 1, 1)
    row_scale = jnp.exp(jax.random.uniform(key_rows, (SECTIONS, TOKENS, 1), minval=0.0, maxval=math.log(10.0))) / 3.0
    base = jax.random.normal(key_base, (SECTIONS, TOKENS, VW), dtype=jnp.float32)
    values = 0.1 * base * section_rise[:, None, None] * column_rise[None, None, :] * row_scale
    return jnp.clip(values, -4.0, 4.0).astype(jnp.bfloat16)


def block_levels(own_key, shape, cuts, least, high):
    def one(dim, parts):
        steps = jax.random.uniform(jax.random.fold_in(jax.random.fold_in(own_key, 6), dim), (parts,), jnp.float32, least / len(cuts), high / len(cuts))
        return jnp.repeat(jnp.exp(steps), shape[dim] // parts).reshape((-1,) + (1,) * (len(shape) - dim - 1))

    loudness = one(*cuts[0])
    for cut in cuts[1:]:
        loudness = loudness * one(*cut)
    return loudness


def gaussian(rng, dims, scale, most, cuts=(), held_as=jnp.bfloat16):
    array = scale * jax.random.normal(rng, dims, jnp.float32)
    if cuts:
        array = array * block_levels(rng, dims, cuts, -0.22, 0.18)
    return jnp.clip(array, -most, most).astype(held_as)


def setup_inputs(seed: int = 0) -> dict:
    key_list = jax.random.split(jax.random.key(seed), 7)
    return {
        "activations": gaussian(key_list[0], (SECTIONS, TOKENS, D), 1.0, 6.0, ((0, 2), (1, 128))),
        "norm_gain": jnp.clip(1.0 + 0.1 * jax.random.normal(key_list[1], (SECTIONS, D), jnp.float32), 0.5, 1.5),
        "value_weight": gaussian(key_list[2], (SECTIONS, D, VW), (VW // 8) ** -0.5, 0.75, ((0, 2), (2, 2))),
        "upstream_grad": draw_upstream_grad(jax.random.fold_in(key_list[6], 71), 0),
        "error_buffer": gaussian(key_list[4], (SECTIONS, ERR_ROWS, VW), 2.0, 12.0, ((0, 2), (1, 64), (2, 2))),
        "prior_basis": gaussian(key_list[5], (SECTIONS, VW, RANK), 1.0, 6.0, ((0, 2), (1, 2)), jnp.float32),
    }


epsilon = 1e-05
clip_level = 0.25

def orthonormal(factor, gram):
    lower = jnp.linalg.cholesky(gram)
    return lax.linalg.triangular_solve(lower, factor, left_side=False, lower=True, transpose_a=True)

def orthonormal_full(factor):
    gram = jnp.dot(factor.T.astype(jnp.float32), factor.astype(jnp.float32), precision=lax.Precision.HIGHEST, preferred_element_type=jnp.float32)
    return orthonormal(factor, gram)

def norm_backward(activ, inverse_rms, gain_vector, feature_grad):
    scaled = gain_vector * feature_grad
    along = lax.optimization_barrier(jnp.mean(activ * scaled, axis=-1, keepdims=True))
    return inverse_rms * scaled - activ * inverse_rms * inverse_rms * inverse_rms * along

def merge_one(items):
    normed_block, upstream_block, error_block = items
    product = jnp.dot(normed_block.T.astype(jnp.float32), upstream_block.astype(jnp.float32), preferred_element_type=jnp.float32)
    return product + error_block.astype(jnp.float32)

def reference(activations, norm_gain, value_weight, upstream_grad, error_buffer, prior_basis):
    section_list = []
    left_list = []
    right_list = []
    error_list = []
    for section_index in range(SECTIONS):
        activ = activations[section_index].astype(jnp.float32)
        gain_vector = norm_gain[section_index]
        inverse_rms = lax.rsqrt(lax.optimization_barrier(jnp.mean(activ * activ, axis=-1, keepdims=True)) + epsilon)
        normed = (activ * inverse_rms * gain_vector).astype(jnp.bfloat16)
        feature_grad = jnp.dot(upstream_grad[section_index].astype(jnp.float32), value_weight[section_index].T.astype(jnp.float32), preferred_element_type=jnp.float32)
        section_list.append(norm_backward(activ, inverse_rms, gain_vector, feature_grad).astype(jnp.bfloat16))
        normed_split = normed.reshape(N_DP, TOK_DEV, D)
        upstream_split = upstream_grad[section_index].reshape(N_DP, TOK_DEV, VW)
        error_split = error_buffer[section_index].reshape(N_DP, D, VW)
        merged = lax.map(merge_one, (normed_split, upstream_split, error_split)).reshape(N_DP, D, N_TENSOR, V_DEV)
        basis = prior_basis[section_index].reshape(N_TENSOR, V_DEV, RANK)
        summed = jnp.einsum('rdtv,tvk->tdk', merged, basis, precision=lax.Precision.HIGHEST)
        left = jax.vmap(orthonormal_full)(summed)
        right = jnp.einsum('rdtv,tdk->tvk', merged, left, precision=lax.Precision.HIGHEST) / N_DP
        approx = jnp.einsum('tdk,tvk->dtv', left, right, precision=lax.Precision.HIGHEST)
        error_list.append((merged - approx[None]).astype(jnp.bfloat16).reshape(N_DP * D, VW))
        left_list.append(left.reshape(N_TENSOR * D, RANK))
        right_list.append(right.reshape(VW, RANK))
    received = jnp.stack(section_list[1:] + [jnp.zeros_like(section_list[0])])
    right_stack = jnp.stack(right_list)
    total = jnp.sum(right_stack * right_stack)
    factor = jnp.minimum(1.0, clip_level * math.sqrt(SECTIONS * VW * RANK) / jnp.sqrt(total + 1e-06))
    return (received, jnp.stack(left_list), right_stack * factor, jnp.stack(error_list))
```

```python
import math

import jax
import jax.numpy as jnp
from jax import lax
from jax.sharding import Mesh, PartitionSpec as P

epsilon = 1e-05
clip_level = 0.25
DP = ("z", "y", "xh")
f32 = jnp.float32
bf16 = jnp.bfloat16


def halves(value):
    high = lax.reduce_precision(value, exponent_bits=8, mantissa_bits=7)
    return high.astype(bf16), (value - high).astype(bf16)


def dot(left, right, left_dim, right_dim):
    return lax.dot_general(
        left, right, (((left_dim,), (right_dim,)), ((), ())), preferred_element_type=f32
    )


def exchange(chunks, axis):
    return lax.all_to_all(chunks, axis, 0, 0, tiled=False)


def spread(value, axis, count):
    return exchange(jnp.broadcast_to(value[None], (count,) + value.shape), axis)


def exact(left, right, left_dim, right_dim):
    return lax.dot_general(
        left,
        right,
        (((left_dim,), (right_dim,)), ((), ())),
        precision=lax.Precision.HIGHEST,
        preferred_element_type=f32,
    )


def local(activations, norm_gain, value_weight, upstream_grad, error_buffer, prior_basis):
    activ_own = activations[0]
    gain = norm_gain[0]
    weights = value_weight[0]
    upstream = upstream_grad[0]
    error = error_buffer[0]
    basis = prior_basis[0]
    tokens, width = activ_own.shape
    columns = upstream.shape[1]
    rank = basis.shape[1]
    shard = lax.axis_index("tensor")
    swap = [(0, 1), (1, 0)]

    up_own = lax.dynamic_slice_in_dim(upstream, shard * tokens, tokens, 0)
    up_give = lax.dynamic_slice_in_dim(upstream, (1 - shard) * tokens, tokens, 0)
    up_other = lax.ppermute(up_give, "tensor", swap)
    basis_other = lax.ppermute(basis, "tensor", swap)

    beside = [(2, 7), (7, 2), (3, 6), (6, 3)]
    weights_other = lax.ppermute(weights, ("xh", "pipe", "tensor"), beside)
    up_other, basis_other, activ_late = lax.optimization_barrier((up_other, basis_other, activ_own))
    activ_other = lax.ppermute(activ_late, "tensor", swap)

    def normalised(rows):
        wide = rows.astype(f32)
        inverse = lax.rsqrt(jnp.mean(wide * wide, axis=-1, keepdims=True) + epsilon)
        return wide, inverse, (wide * inverse * gain).astype(bf16)

    activ, inverse_rms, normed_own = normalised(activ_own)

    basis_parts = jnp.concatenate(halves(basis), axis=1)
    from_error = dot(basis_parts, error, 0, 1)
    from_error = from_error[:rank] + from_error[rank:]
    own_v = exact(basis, up_own.astype(f32), 0, 1)
    other_v = exact(basis_other, up_other.astype(f32), 0, 1)
    both_v = jnp.concatenate([own_v, other_v], axis=0)
    product = dot(jnp.concatenate(halves(both_v), axis=0), normed_own, 1, 0)
    product = product[: 2 * rank] + product[2 * rank :]
    own_p = product[:rank] + from_error
    other_p = product[rank:]
    first = jnp.where(shard == 0, own_p, other_p)
    second = jnp.where(shard == 0, other_p, own_p)
    terms = jnp.concatenate([first, second], axis=0)

    n_y, n_z, n_x = lax.axis_size("y"), lax.axis_size("z"), lax.axis_size("xh")
    n_t = lax.axis_size("tensor")
    part_y = width // n_y
    part_z = part_y // n_z
    terms = terms.reshape(n_t * rank, n_y, part_y).transpose(1, 0, 2)
    terms = exchange(terms, "y").sum(0)
    terms = terms.reshape(n_t * rank, n_z, part_z).transpose(1, 0, 2)
    terms = exchange(terms, "z").sum(0).reshape(1, n_t, rank, part_z)
    terms = jnp.broadcast_to(terms, (n_x, n_t, rank, part_z)).reshape(n_x * n_t, rank, part_z)
    summed = exchange(terms, ("xh", "tensor")).sum(0)
    summed = spread(summed, "z", n_z).transpose(1, 0, 2).reshape(rank, part_y)
    summed = spread(summed, "y", n_y).transpose(1, 0, 2).reshape(rank, width)

    _, _, normed_other = normalised(activ_other)
    low = jnp.where(shard == 0, normed_own, normed_other)
    high = jnp.where(shard == 0, normed_other, normed_own)
    normed = jnp.concatenate([low, high], axis=0)
    merged = dot(normed, upstream, 0, 0) + error.astype(f32)

    summed_parts = jnp.concatenate(halves(summed), axis=0)
    from_tokens = dot(summed_parts, normed, 1, 1)
    from_tokens = from_tokens[:rank] + from_tokens[rank:]
    direct = dot(summed_parts, error, 1, 0)
    local_right = direct[:rank] + direct[rank:]
    through = dot(jnp.concatenate(halves(from_tokens), axis=0), upstream, 1, 0)
    local_right = local_right + through[:rank] + through[rank:]

    right_terms = spread(local_right, ("y", "xh"), n_y * n_x).sum(0)
    right_sum = spread(right_terms, "z", n_z).sum(0)

    gram = exact(summed, summed, 1, 1)
    lower = jnp.linalg.cholesky(gram)
    left = lax.linalg.triangular_solve(lower, summed, left_side=True, lower=True)
    mean_right = lax.linalg.triangular_solve(lower, right_sum, left_side=True, lower=True)
    mean_right = mean_right / (n_y * n_z * n_x)

    left_high, left_low = halves(left)
    right_high, right_low = halves(mean_right)
    approx = dot(
        jnp.concatenate([left_high, left_low, left_high], axis=0),
        jnp.concatenate([right_high, right_high, right_low], axis=0),
        0,
        0,
    )
    error_next = (merged - approx).astype(bf16)

    squares = jnp.sum(mean_right * mean_right)[None, None]
    squares = squares + lax.ppermute(squares, "pipe", swap)
    total = (squares + lax.ppermute(squares, "tensor", swap))[0, 0]
    entries = mean_right.size * lax.axis_size("pipe") * n_t
    factor = jnp.minimum(1.0, clip_level * math.sqrt(entries) / jnp.sqrt(total + 1e-06))

    feature_grad = dot(up_own, weights, 1, 1) + dot(up_other, weights_other, 1, 1)
    scaled = gain * feature_grad
    along = jnp.mean(activ * scaled, axis=-1, keepdims=True)
    section_grad = (
        inverse_rms * scaled - activ * inverse_rms * inverse_rms * inverse_rms * along
    ).astype(bf16)
    received = lax.ppermute(section_grad, "pipe", [(1, 0)])
    return (
        received[None],
        left.T[None],
        (mean_right * factor).T[None],
        error_next[None],
    )


def solution(mesh):
    sizes = (8, 4, 2) if mesh.shape["dp"] == 64 else (mesh.shape["dp"], 1, 1)
    inner = Mesh(
        mesh.devices.reshape(sizes + (mesh.shape["pipe"], mesh.shape["tensor"])),
        DP + ("pipe", "tensor"),
    )
    return jax.shard_map(
        local,
        mesh=inner,
        in_specs=(
            P("pipe", DP + ("tensor",), None),
            P("pipe", None),
            P("pipe", None, "tensor"),
            P("pipe", DP, "tensor"),
            P("pipe", DP, "tensor"),
            P("pipe", "tensor", None),
        ),
        out_specs=(
            P("pipe", DP + ("tensor",), None),
            P("pipe", "tensor", None),
            P("pipe", "tensor", None),
            P("pipe", DP, "tensor"),
        ),
        check_vma=False,
    )
```

```python
import functools
import math

import jax
import jax.numpy as jnp
from jax import lax
from jax.experimental import pallas as pl
from jax.experimental.pallas import tpu as pltpu
from jax.sharding import Mesh, PartitionSpec as P

epsilon = 1e-05
clip_level = 0.25
DP = ("z", "y", "xh")
f32 = jnp.float32
bf16 = jnp.bfloat16
WIRE = f32
SWAP = [(0, 1), (1, 0)]
LIMIT = 60 * 1024 * 1024


def dot(left, right, left_dim, right_dim, precision=None):
    return lax.dot_general(
        left,
        right,
        (((left_dim,), (right_dim,)), ((), ())),
        precision=precision,
        preferred_element_type=f32,
    )


def exact(left, right, left_dim, right_dim):
    return dot(left, right, left_dim, right_dim, lax.Precision.HIGHEST)


def pieces(value, count):
    found = []
    for _ in range(count - 1):
        part = value.astype(bf16)
        found.append(part)
        value = value - part.astype(f32)
    found.append(value.astype(bf16))
    return found


def exchange(chunks, axis):
    return lax.all_to_all(chunks, axis, 0, 0, tiled=False)


def added(terms):
    return terms.astype(f32).sum(0).astype(terms.dtype)


class Stream:
    def __init__(self, far, near, done, dim, parts, begin=0):
        self.far, self.near, self.done, self.dim, self.parts = far, near, done, dim, parts
        self.size = near.shape[dim] // parts
        self.begin = begin
        self.waited = set()

    def place(self, part, begin=0):
        return (slice(None),) * self.dim + (pl.ds(begin + part * self.size, self.size),)

    def bring(self, part):
        source = self.far.at[self.place(part, self.begin)]
        return pltpu.make_async_copy(source, self.near.at[self.place(part)], self.done.at[part])

    def send(self, part):
        place = self.place(part)
        return pltpu.make_async_copy(self.near.at[place], self.far.at[place], self.done.at[part])

    def __call__(self, part=0):
        if part not in self.waited:
            self.bring(part).wait()
            self.waited.add(part)
        return self.near.at[self.place(part)]

    def all(self):
        for part in range(self.parts):
            self(part)
        return self.near

    def out(self, part=0):
        return self.near.at[self.place(part)]


def call(kernel, ins, outs, scratch=(), scalar=None, limit=LIMIT):
    n_in, n_out = len(ins), len(outs)
    scalars = [] if scalar is None else [scalar]

    def body(*refs):
        refs = list(refs)
        front = [refs.pop(0)[0] for _ in scalars]
        far, refs = refs[: n_in + n_out], refs[n_in + n_out :]
        own, refs = refs[: len(scratch)], refs[len(scratch) :]
        near, done = refs[: n_in + n_out], refs[n_in + n_out :]
        marks = [item[1:4] for item in ins]
        marks += [(dim, parts) for _, _, dim, parts in outs]
        streams = [Stream(*item, *mark) for *item, mark in zip(far, near, done, marks)]
        sources, targets = streams[:n_in], streams[n_in:]
        for part in range(max(source.parts for source in sources)):
            for source in sources:
                if part < source.parts:
                    source.bring(part).start()
        kernel(*front, *sources, *targets, *own)
        for source in sources:
            source.all()
        for target in targets:
            for part in range(target.parts):
                target.send(part).wait()

    shapes = []
    for array, dim, parts, *cut in ins:
        shape = list(array.shape)
        if cut:
            shape[dim] = cut[1]
        shapes.append((tuple(shape), array.dtype, parts))
    shapes += [(shape, dtype, parts) for shape, dtype, _, parts in outs]
    found = pl.pallas_call(
        body,
        out_shape=tuple(jax.ShapeDtypeStruct(shape, dtype) for shape, dtype, _, _ in outs),
        in_specs=[pl.BlockSpec(memory_space=pltpu.SMEM) for _ in scalars]
        + [pl.BlockSpec(memory_space=pl.ANY) for _ in ins],
        out_specs=tuple(pl.BlockSpec(memory_space=pl.ANY) for _ in outs),
        scratch_shapes=list(scratch)
        + [pltpu.VMEM(shape, dtype) for shape, dtype, _ in shapes]
        + [pltpu.SemaphoreType.DMA((parts,)) for _, _, parts in shapes],
        compiler_params=pltpu.CompilerParams(vmem_limit_bytes=limit),
        cost_estimate=pl.CostEstimate(flops=0, bytes_accessed=0, transcendentals=0),
    )(*scalars, *[item[0] for item in ins])
    return found if n_out > 1 else found[0]


def normed_of(rows, inverse, gain):
    return (rows * inverse * gain).astype(bf16)


def inverse_of(rows):
    return lax.rsqrt(jnp.mean(rows * rows, axis=-1, keepdims=True) + epsilon)


def half(shard, size):
    return pl.ds(pl.multiple_of(shard * size, size), size)


def projected_kernel(shard, upstream, basis, own_out, give_out, rows_out):
    rank, tokens = own_out.near.shape
    upstream()
    rows_out.near = upstream.near.at[half(1 - shard, tokens)]
    rows_out.send(0).start()
    parts = jnp.concatenate(pieces(basis()[...], 2), axis=0)
    for out, side in ((give_out, 1 - shard), (own_out, shard)):
        both = dot(parts, upstream()[half(side, tokens), :], 1, 1)
        out.out()[...] = both[:rank] + both[rank:]
        out.send(0).start()


def terms_kernel(shard, activ, gain, error, basis, own_v, other_v, normed, out):
    rank = basis.near.shape[0]
    lanes = out.near.shape[-1]
    for part in range(activ.parts):
        rows = activ(part)[...].astype(f32)
        normed.out(part)[...] = normed_of(rows, inverse_of(rows), gain()[...])
        normed.send(part).start()
    pair = jnp.concatenate(pieces(basis()[...], 2), axis=0)
    both = jnp.concatenate([own_v()[...], other_v()[...]], axis=0)
    both = jnp.concatenate(pieces(both, 2), axis=0)
    for part in range(error.parts):
        columns = slice(part * error.size, (part + 1) * error.size)
        product = dot(both, normed.near[:, columns], 1, 0)
        product = product[: 2 * rank] + product[2 * rank :]
        from_error = dot(pair, error(part)[...], 1, 1)
        own = product[:rank] + (from_error[:rank] + from_error[rank:])
        other = product[rank:]
        for chunk in range(out.size):
            columns = slice(chunk * lanes, (chunk + 1) * lanes)
            out.out(part)[chunk, shard] = own[:, columns].astype(out.near.dtype)
            out.out(part)[chunk, 1 - shard] = other[:, columns].astype(out.near.dtype)
        out.send(part).start()


def split_out(out, part, value):
    high, low = pieces(value, 2)
    columns = value.shape[1]
    out.out(part)[:, :columns] = high
    out.out(part)[:, columns:] = low
    out.send(part).start()


def joined(both):
    columns = both.shape[1] // 2
    return both[:, :columns].astype(f32) + both[:, columns:].astype(f32)


def own_kernel(shard, normed, upstream, error, out):
    rows = upstream()[half(shard, normed.near.shape[0]), :]
    for part in range(out.parts):
        split_out(out, part, dot(normed(part)[...], rows, 0, 0) + error(part)[...].astype(f32))


def merged_kernel(shard, activ, gain, upstream, own, out, inverse):
    rows = upstream()[half(1 - shard, activ.near.shape[0]), :]
    for part in range(activ.parts):
        place = pl.ds(part * activ.size, activ.size)
        inverse[place, :] = inverse_of(activ(part)[...].astype(f32))
    for part in range(out.parts):
        lanes = slice(part * out.size, (part + 1) * out.size)
        other = normed_of(activ.near[:, lanes].astype(f32), inverse[...], gain()[:, lanes])
        split_out(out, part, dot(other, rows, 0, 0) + joined(own(part)[...]))


def right_kernel(summed, merged, right_out, gram_out):
    rank = summed.near.shape[1]
    columns = merged.near.shape[1] // 2
    gram = right = 0.0
    for part in range(summed.parts):
        chunk = summed(part)
        whole = jnp.concatenate([chunk[i].astype(f32) for i in range(summed.size)], axis=1)
        parts = jnp.concatenate(pieces(whole, 3), axis=0)
        gram = gram + dot(parts, parts, 1, 1)
        right = right + dot(parts, merged(part)[...], 1, 0)
    right = right[:, :columns] + right[:, columns:]
    right = right[:rank] + right[rank : 2 * rank] + right[2 * rank :]
    right_out.out()[...] = jnp.broadcast_to(right[None], right_out.near.shape)
    right_out.send(0).start()
    gram = gram[:rank] + gram[rank : 2 * rank] + gram[2 * rank :]
    gram_out.out()[...] = gram[:, :rank] + gram[:, rank : 2 * rank] + gram[:, 2 * rank :]
    gram_out.send(0).start()


def left_kernel(gram, summed, left_out, parts_out, inverse_out, inverse):
    rank = gram.near.shape[0]
    row = lax.broadcasted_iota(jnp.int32, (rank, rank), 0)
    column = lax.broadcasted_iota(jnp.int32, (rank, rank), 1)
    both = jnp.concatenate([gram()[...], jnp.where(row == column, 1.0, 0.0)], axis=1)
    below = lax.broadcasted_iota(jnp.int32, (rank, 1), 0)
    for k in range(rank):
        scale = lax.rsqrt(both[k : k + 1, k : k + 1])
        pivot = both[k : k + 1, :] * scale
        inverse[k : k + 1, :] = pivot[:, rank:]
        factor = jnp.where(below > k, both[:, k : k + 1] * scale, 0.0)
        both = both - factor * pivot
    inverse_out.out()[...] = inverse[...]
    inverse_out.send(0).start()
    lanes = summed.near.shape[2] * summed.size
    for part in range(summed.parts):
        chunk = summed(part)
        whole = jnp.concatenate([chunk[i].astype(f32) for i in range(summed.size)], axis=1)
        left = exact(inverse[...], whole, 1, 0)
        left_out.out(part)[...] = left
        left_out.send(part).start()
        high, low = pieces(left, 2)
        parts_out.out(part)[...] = jnp.concatenate([high, low, high, high], axis=0).T
        parts_out.send(part).start()


def mean_kernel(terms, inverse, mean_out, parts_out, squares_out, *, replicas):
    total = jnp.sum(terms()[...], axis=0)
    mean = exact(inverse()[...], total, 1, 0) * (1.0 / replicas)
    squares = jnp.sum(jnp.sum(mean * mean, axis=1, keepdims=True), axis=0, keepdims=True)
    squares_out.out()[...] = jnp.broadcast_to(squares, squares_out.near.shape)
    squares_out.send(0).start()
    high, low = pieces(mean, 2)
    parts_out.out()[...] = jnp.concatenate([high, high, low, jnp.zeros_like(low)], axis=0)
    parts_out.send(0).start()
    mean_out.out()[...] = mean
    mean_out.send(0).start()


def error_kernel(merged, left, right, out):
    few = 128
    for part in range(out.parts):
        for start in range(0, out.size, few):
            rows = slice(start, start + few)
            approx = dot(left(part)[rows, :], right()[...], 1, 0)
            out.out(part)[rows, :] = (joined(merged(part)[rows, :]) - approx).astype(bf16)
        out.send(part).start()


def section_kernel(shard, activ, gain, upstream, other, weights, beside, *refs):
    out, scaled = refs
    tokens, width = activ.near.shape
    own = upstream()[half(shard, tokens), :]
    squares = along = 0.0
    for part in range(weights.parts):
        lanes = slice(part * weights.size, (part + 1) * weights.size)
        rows = activ()[:, lanes].astype(f32)
        product = dot(own, weights(part)[...], 1, 1) + dot(other()[...], beside(part)[...], 1, 1)
        product = product * gain()[:, lanes]
        scaled[:, lanes] = product
        squares = squares + jnp.sum(rows * rows, axis=-1, keepdims=True)
        along = along + jnp.sum(rows * product, axis=-1, keepdims=True)
    inverse = lax.rsqrt(squares * (1.0 / width) + epsilon)
    along = along * (1.0 / width) * inverse * inverse * inverse
    few = tokens // out.parts
    for part in range(out.parts):
        rows = slice(part * few, (part + 1) * few)
        value = inverse[rows] * scaled[rows, :] - activ()[rows, :].astype(f32) * along[rows]
        out.out(part)[...] = value.astype(bf16)
        out.send(part).start()


def local(activations, norm_gain, value_weight, upstream_grad, error_buffer, prior_basis):
    activ_own = activations[0]
    weights = value_weight[0]
    upstream = upstream_grad[0]
    error = error_buffer[0]
    basis = prior_basis[0].T
    tokens, width = activ_own.shape
    replica_tokens, columns = upstream.shape
    rank = basis.shape[0]
    shard = lax.axis_index("tensor")
    where = shard.astype(jnp.int32).reshape(1)
    n_y, n_z, n_x = lax.axis_size("y"), lax.axis_size("z"), lax.axis_size("xh")
    n_t, n_p = lax.axis_size("tensor"), lax.axis_size("pipe")
    replicas = n_y * n_z * n_x
    lanes = width // (n_z * n_y)
    steps = 8

    own_v, give_v, up_give = call(
        projected_kernel,
        [(upstream, 0, 1), (basis, 0, 1)],
        [((rank, tokens), f32, 0, 1)] * 2 + [((tokens, columns), bf16, 0, 1)],
        scalar=where,
    )
    other_v = lax.ppermute(give_v, "tensor", SWAP)
    up_other = lax.ppermute(up_give, ("pipe", "tensor"), [(2, 3), (3, 2)])

    other_v, up_other, activ_late, weights_late = lax.optimization_barrier(
        (other_v, up_other, activ_own, weights)
    )
    activ_other = lax.ppermute(activ_late, "tensor", SWAP)
    beside = [(2, 7), (7, 2), (3, 6), (6, 3)]
    weights_other = lax.ppermute(weights_late, ("xh", "pipe", "tensor"), beside)
    normed_own, terms = call(
        terms_kernel,
        [
            (activ_late, 0, 4),
            (norm_gain, 0, 1),
            (error, 0, 4),
            (basis, 0, 1),
            (own_v, 0, 1),
            (other_v, 0, 1),
        ],
        [((tokens, width), bf16, 0, 4), ((n_y * n_z, n_t, rank, lanes), WIRE, 0, 4)],
        scalar=where,
    )
    terms = terms.reshape(n_y * n_z, n_t * rank, lanes)
    terms, activ_late, normed_late = lax.optimization_barrier((terms, activ_own, normed_own))
    terms = exchange(terms, ("y", "z"))
    section_grad = call(
        section_kernel,
        [
            (activ_late, 0, 1),
            (norm_gain, 0, 1),
            (upstream, 0, 1),
            (up_other, 0, 1),
            (weights, 0, steps),
            (weights_other, 0, steps),
        ],
        [((tokens, width), bf16, 0, 4)],
        scratch=[pltpu.VMEM((tokens, width), f32)],
        scalar=where,
    )
    own = call(
        own_kernel,
        [(normed_late, 1, 4), (upstream, 0, 1), (error, 0, 4)],
        [((width, 2 * columns), bf16, 0, 4)],
        scalar=where,
    )
    received = lax.ppermute(section_grad, "pipe", [(1, 0)])
    terms, activ_other, own = lax.optimization_barrier((terms, activ_other, own))
    terms = added(terms).reshape(1, n_t, rank, lanes)
    terms = jnp.broadcast_to(terms, (n_x, n_t, rank, lanes)).reshape(n_x * n_t, rank, lanes)
    summed = added(exchange(terms, ("xh", "tensor")))
    summed = exchange(jnp.broadcast_to(summed[None], (n_z,) + summed.shape), "z")
    summed, received, own = lax.optimization_barrier((summed, received, own))
    summed = exchange(jnp.broadcast_to(summed[None], (n_y,) + summed.shape), "y")
    merged = call(
        merged_kernel,
        [
            (activ_other, 0, 4),
            (norm_gain, 0, 1),
            (upstream, 0, 1),
            (own, 0, 4),
        ],
        [((width, 2 * columns), bf16, 0, 4)],
        scratch=[pltpu.VMEM((tokens, 1), f32)],
        scalar=where,
    )
    summed, merged = lax.optimization_barrier((summed, merged))
    summed = summed.reshape(n_y * n_z, rank, lanes)
    near = n_y * n_x
    right_terms, gram = call(
        right_kernel,
        [(summed, 0, 4), (merged, 0, 4)],
        [((near, rank, columns), f32, 0, 1), ((rank, rank), f32, 0, 1)],
    )
    right_terms = exchange(right_terms, ("y", "xh"))
    left, left_parts, inverse = call(
        left_kernel,
        [(gram, 0, 1), (summed, 0, 4)],
        [
            ((rank, width), f32, 1, 4),
            ((width, 4 * rank), bf16, 0, 4),
            ((rank, rank), f32, 0, 1),
        ],
        scratch=[pltpu.VMEM((rank, rank), f32)],
    )
    right_terms, left, left_parts, inverse, received = lax.optimization_barrier(
        (right_terms, left, left_parts, inverse, received)
    )
    last = lax.axis_index("pipe") == n_p - 1
    received = jnp.where(last, jnp.zeros_like(received), received)
    right_terms = jnp.broadcast_to(right_terms.sum(0)[None], (n_z, rank, columns))
    right_terms = exchange(right_terms, "z")
    right_terms, received = lax.optimization_barrier((right_terms, received))
    mean_right, right_parts, squares = call(
        functools.partial(mean_kernel, replicas=replicas),
        [(right_terms, 0, 1), (inverse, 0, 1)],
        [
            ((rank, columns), f32, 0, 1),
            ((4 * rank, columns), bf16, 0, 1),
            ((rank, columns), f32, 0, 1),
        ],
        limit=8 * 1024 * 1024,
    )
    total = (
        squares
        + lax.ppermute(squares, "pipe", SWAP)
        + lax.ppermute(squares, "tensor", SWAP)
        + lax.ppermute(squares, ("pipe", "tensor"), [(0, 3), (3, 0), (1, 2), (2, 1)])
    )
    error_next = call(
        error_kernel,
        [
            (merged, 0, 4),
            (left_parts, 0, 4),
            (right_parts, 0, 1),
        ],
        [((width, columns), bf16, 0, 4)],
    )
    entries = mean_right.size * n_p * n_t
    factor = jnp.minimum(1.0, clip_level * math.sqrt(entries) / jnp.sqrt(total + 1e-06))
    return (
        received[None],
        left.T[None],
        (mean_right * factor).T[None],
        error_next[None],
    )


def solution(mesh):
    inner = Mesh(
        mesh.devices.reshape((8, 4, 2, mesh.shape["pipe"], mesh.shape["tensor"])),
        DP + ("pipe", "tensor"),
    )
    return jax.shard_map(
        local,
        mesh=inner,
        in_specs=(
            P("pipe", DP + ("tensor",), None),
            P("pipe", None),
            P("pipe", None, "tensor"),
            P("pipe", DP, "tensor"),
            P("pipe", DP, "tensor"),
            P("pipe", "tensor", None),
        ),
        out_specs=(
            P("pipe", DP + ("tensor",), None),
            P("pipe", "tensor", None),
            P("pipe", "tensor", None),
            P("pipe", DP, "tensor"),
        ),
        check_vma=False,
    )
```

```python
import functools
import math

import jax
import jax.numpy as jnp
from jax import lax
from jax.experimental import pallas as pl
from jax.experimental.pallas import tpu as pltpu
from jax.sharding import Mesh, PartitionSpec as P

epsilon = 1e-05
clip_level = 0.25
DP = ("z", "y", "xh")
f32 = jnp.float32
bf16 = jnp.bfloat16
WIRE = f32
SWAP = [(0, 1), (1, 0)]
LIMIT = 60 * 1024 * 1024


def dot(left, right, left_dim, right_dim, precision=None):
    return lax.dot_general(
        left,
        right,
        (((left_dim,), (right_dim,)), ((), ())),
        precision=precision,
        preferred_element_type=f32,
    )


def exact(left, right, left_dim, right_dim):
    return dot(left, right, left_dim, right_dim, lax.Precision.HIGHEST)


def pieces(value, count):
    found = []
    for _ in range(count - 1):
        part = value.astype(bf16)
        found.append(part)
        value = value - part.astype(f32)
    found.append(value.astype(bf16))
    return found


def exchange(chunks, axis):
    return lax.all_to_all(chunks, axis, 0, 0, tiled=False)


def added(terms):
    return terms.astype(f32).sum(0).astype(terms.dtype)


class Stream:
    def __init__(self, far, near, done, dim, parts, begin=0):
        self.far, self.near, self.done, self.dim, self.parts = far, near, done, dim, parts
        self.size = near.shape[dim] // parts
        self.begin = begin
        self.waited = set()

    def place(self, part, begin=0):
        return (slice(None),) * self.dim + (pl.ds(begin + part * self.size, self.size),)

    def bring(self, part):
        source = self.far.at[self.place(part, self.begin)]
        return pltpu.make_async_copy(source, self.near.at[self.place(part)], self.done.at[part])

    def send(self, part):
        place = self.place(part)
        return pltpu.make_async_copy(self.near.at[place], self.far.at[place], self.done.at[part])

    def __call__(self, part=0):
        if part not in self.waited:
            self.bring(part).wait()
            self.waited.add(part)
        return self.near.at[self.place(part)]

    def all(self):
        for part in range(self.parts):
            self(part)
        return self.near

    def out(self, part=0):
        return self.near.at[self.place(part)]


def call(kernel, ins, outs, scratch=(), scalar=None, limit=LIMIT):
    n_in, n_out = len(ins), len(outs)
    scalars = [] if scalar is None else [scalar]

    def body(*refs):
        refs = list(refs)
        front = [refs.pop(0)[0] for _ in scalars]
        far, refs = refs[: n_in + n_out], refs[n_in + n_out :]
        own, refs = refs[: len(scratch)], refs[len(scratch) :]
        near, done = refs[: n_in + n_out], refs[n_in + n_out :]
        marks = [item[1:4] for item in ins]
        marks += [(dim, parts) for _, _, dim, parts in outs]
        streams = [Stream(*item, *mark) for *item, mark in zip(far, near, done, marks)]
        sources, targets = streams[:n_in], streams[n_in:]
        for part in range(max(source.parts for source in sources)):
            for source in sources:
                if part < source.parts:
                    source.bring(part).start()
        kernel(*front, *sources, *targets, *own)
        for source in sources:
            source.all()
        for target in targets:
            for part in range(target.parts):
                target.send(part).wait()

    shapes = []
    for array, dim, parts, *cut in ins:
        shape = list(array.shape)
        if cut:
            shape[dim] = cut[1]
        shapes.append((tuple(shape), array.dtype, parts))
    shapes += [(shape, dtype, parts) for shape, dtype, _, parts in outs]
    found = pl.pallas_call(
        body,
        out_shape=tuple(jax.ShapeDtypeStruct(shape, dtype) for shape, dtype, _, _ in outs),
        in_specs=[pl.BlockSpec(memory_space=pltpu.SMEM) for _ in scalars]
        + [pl.BlockSpec(memory_space=pl.ANY) for _ in ins],
        out_specs=tuple(pl.BlockSpec(memory_space=pl.ANY) for _ in outs),
        scratch_shapes=list(scratch)
        + [pltpu.VMEM(shape, dtype) for shape, dtype, _ in shapes]
        + [pltpu.SemaphoreType.DMA((parts,)) for _, _, parts in shapes],
        compiler_params=pltpu.CompilerParams(vmem_limit_bytes=limit),
        cost_estimate=pl.CostEstimate(flops=0, bytes_accessed=0, transcendentals=0),
    )(*scalars, *[item[0] for item in ins])
    return found if n_out > 1 else found[0]


def normed_of(rows, inverse, gain):
    return (rows * inverse * gain).astype(bf16)


def inverse_of(rows):
    return lax.rsqrt(jnp.mean(rows * rows, axis=-1, keepdims=True) + epsilon)


def half(shard, size):
    return pl.ds(pl.multiple_of(shard * size, size), size)


def projected_kernel(shard, upstream, basis, own_out, give_out, rows_out):
    rank, tokens = own_out.near.shape
    upstream()
    rows_out.near = upstream.near.at[half(1 - shard, tokens)]
    rows_out.send(0).start()
    parts = jnp.concatenate(pieces(basis()[...], 2), axis=0)
    for out, side in ((give_out, 1 - shard), (own_out, shard)):
        both = dot(parts, upstream()[half(side, tokens), :], 1, 1)
        out.out()[...] = both[:rank] + both[rank:]
        out.send(0).start()


def terms_kernel(shard, activ, gain, error, basis, own_v, other_v, normed, out):
    rank = basis.near.shape[0]
    lanes = out.near.shape[-1]
    for part in range(activ.parts):
        rows = activ(part)[...].astype(f32)
        normed.out(part)[...] = normed_of(rows, inverse_of(rows), gain()[...])
        normed.send(part).start()
    pair = jnp.concatenate(pieces(basis()[...], 2), axis=0)
    both = jnp.concatenate([own_v()[...], other_v()[...]], axis=0)
    both = jnp.concatenate(pieces(both, 2), axis=0)
    for part in range(error.parts):
        columns = slice(part * error.size, (part + 1) * error.size)
        product = dot(both, normed.near[:, columns], 1, 0)
        product = product[: 2 * rank] + product[2 * rank :]
        from_error = dot(pair, error(part)[...], 1, 1)
        own = product[:rank] + (from_error[:rank] + from_error[rank:])
        other = product[rank:]
        for chunk in range(out.size):
            columns = slice(chunk * lanes, (chunk + 1) * lanes)
            out.out(part)[chunk, shard] = own[:, columns].astype(out.near.dtype)
            out.out(part)[chunk, 1 - shard] = other[:, columns].astype(out.near.dtype)
        out.send(part).start()


def split_out(out, part, value):
    high, low = pieces(value, 2)
    columns = value.shape[1]
    out.out(part)[:, :columns] = high
    out.out(part)[:, columns:] = low
    out.send(part).start()


def joined(both):
    columns = both.shape[1] // 2
    return both[:, :columns].astype(f32) + both[:, columns:].astype(f32)


def own_kernel(shard, normed, upstream, error, out):
    rows = upstream()[half(shard, normed.near.shape[0]), :]
    for part in range(out.parts):
        split_out(out, part, dot(normed(part)[...], rows, 0, 0) + error(part)[...].astype(f32))


def merged_kernel(shard, activ, gain, upstream, own, out, inverse):
    rows = upstream()[half(1 - shard, activ.near.shape[0]), :]
    for part in range(activ.parts):
        place = pl.ds(part * activ.size, activ.size)
        inverse[place, :] = inverse_of(activ(part)[...].astype(f32))
    for part in range(out.parts):
        lanes = slice(part * out.size, (part + 1) * out.size)
        other = normed_of(activ.near[:, lanes].astype(f32), inverse[...], gain()[:, lanes])
        split_out(out, part, dot(other, rows, 0, 0) + joined(own(part)[...]))


def right_kernel(summed, merged, right_out, gram_out):
    rank = summed.near.shape[1]
    columns = merged.near.shape[1] // 2
    gram = right = 0.0
    for part in range(summed.parts):
        chunk = summed(part)
        whole = jnp.concatenate([chunk[i].astype(f32) for i in range(summed.size)], axis=1)
        parts = jnp.concatenate(pieces(whole, 3), axis=0)
        gram = gram + dot(parts, parts, 1, 1)
        right = right + dot(parts, merged(part)[...], 1, 0)
    right = right[:, :columns] + right[:, columns:]
    right = right[:rank] + right[rank : 2 * rank] + right[2 * rank :]
    right_out.out()[...] = jnp.broadcast_to(right[None], right_out.near.shape)
    right_out.send(0).start()
    gram = gram[:rank] + gram[rank : 2 * rank] + gram[2 * rank :]
    gram_out.out()[...] = gram[:, :rank] + gram[:, rank : 2 * rank] + gram[:, 2 * rank :]
    gram_out.send(0).start()


def left_kernel(gram, summed, left_out, parts_out, inverse_out, inverse):
    rank = gram.near.shape[0]
    row = lax.broadcasted_iota(jnp.int32, (rank, rank), 0)
    column = lax.broadcasted_iota(jnp.int32, (rank, rank), 1)
    both = jnp.concatenate([gram()[...], jnp.where(row == column, 1.0, 0.0)], axis=1)
    below = lax.broadcasted_iota(jnp.int32, (rank, 1), 0)
    for k in range(rank):
        scale = lax.rsqrt(both[k : k + 1, k : k + 1])
        pivot = both[k : k + 1, :] * scale
        inverse[k : k + 1, :] = pivot[:, rank:]
        factor = jnp.where(below > k, both[:, k : k + 1] * scale, 0.0)
        both = both - factor * pivot
    inverse_out.out()[...] = inverse[...]
    inverse_out.send(0).start()
    lanes = summed.near.shape[2] * summed.size
    for part in range(summed.parts):
        chunk = summed(part)
        whole = jnp.concatenate([chunk[i].astype(f32) for i in range(summed.size)], axis=1)
        left = exact(inverse[...], whole, 1, 0)
        left_out.out(part)[...] = left
        left_out.send(part).start()
        high, low = pieces(left, 2)
        parts_out.out(part)[...] = jnp.concatenate([high, low, high, high], axis=0).T
        parts_out.send(part).start()


def mean_kernel(terms, inverse, mean_out, parts_out, squares_out, *, replicas):
    total = jnp.sum(terms()[...], axis=0)
    mean = exact(inverse()[...], total, 1, 0) * (1.0 / replicas)
    squares = jnp.sum(jnp.sum(mean * mean, axis=1, keepdims=True), axis=0, keepdims=True)
    squares_out.out()[...] = jnp.broadcast_to(squares, squares_out.near.shape)
    squares_out.send(0).start()
    high, low = pieces(mean, 2)
    parts_out.out()[...] = jnp.concatenate([high, high, low, jnp.zeros_like(low)], axis=0)
    parts_out.send(0).start()
    mean_out.out()[...] = mean
    mean_out.send(0).start()


def error_kernel(merged, left, right, out):
    few = 128
    for part in range(out.parts):
        for start in range(0, out.size, few):
            rows = slice(start, start + few)
            approx = dot(left(part)[rows, :], right()[...], 1, 0)
            out.out(part)[rows, :] = (joined(merged(part)[rows, :]) - approx).astype(bf16)
        out.send(part).start()


def section_kernel(shard, activ, gain, upstream, other, weights, beside, *refs):
    out, scaled = refs
    tokens, width = activ.near.shape
    own = upstream()[half(shard, tokens), :]
    squares = along = 0.0
    for part in range(weights.parts):
        lanes = slice(part * weights.size, (part + 1) * weights.size)
        rows = activ()[:, lanes].astype(f32)
        product = dot(own, weights(part)[...], 1, 1) + dot(other()[...], beside(part)[...], 1, 1)
        product = product * gain()[:, lanes]
        scaled[:, lanes] = product
        squares = squares + jnp.sum(rows * rows, axis=-1, keepdims=True)
        along = along + jnp.sum(rows * product, axis=-1, keepdims=True)
    inverse = lax.rsqrt(squares * (1.0 / width) + epsilon)
    along = along * (1.0 / width) * inverse * inverse * inverse
    few = tokens // out.parts
    for part in range(out.parts):
        rows = slice(part * few, (part + 1) * few)
        value = inverse[rows] * scaled[rows, :] - activ()[rows, :].astype(f32) * along[rows]
        out.out(part)[...] = value.astype(bf16)
        out.send(part).start()


def local(activations, norm_gain, value_weight, upstream_grad, error_buffer, prior_basis):
    activ_own = activations[0]
    weights = value_weight[0]
    upstream = upstream_grad[0]
    error = error_buffer[0]
    basis = prior_basis[0].T
    tokens, width = activ_own.shape
    replica_tokens, columns = upstream.shape
    rank = basis.shape[0]
    shard = lax.axis_index("tensor")
    where = shard.astype(jnp.int32).reshape(1)
    n_y, n_z, n_x = lax.axis_size("y"), lax.axis_size("z"), lax.axis_size("xh")
    n_t, n_p = lax.axis_size("tensor"), lax.axis_size("pipe")
    replicas = n_y * n_z * n_x
    lanes = width // (n_z * n_y)
    steps = 8

    own_v, give_v, up_give = call(
        projected_kernel,
        [(upstream, 0, 1), (basis, 0, 1)],
        [((rank, tokens), f32, 0, 1)] * 2 + [((tokens, columns), bf16, 0, 1)],
        scalar=where,
    )
    other_v = lax.ppermute(give_v, "tensor", SWAP)
    up_other = lax.ppermute(up_give, ("pipe", "tensor"), [(2, 3), (3, 2)])

    other_v, up_other, activ_late, weights_late = lax.optimization_barrier(
        (other_v, up_other, activ_own, weights)
    )
    activ_other = lax.ppermute(activ_late, "tensor", SWAP)
    beside = [(2, 7), (7, 2), (3, 6), (6, 3)]
    weights_other = lax.ppermute(weights_late, ("xh", "pipe", "tensor"), beside)
    normed_own, terms = call(
        terms_kernel,
        [
            (activ_late, 0, 4),
            (norm_gain, 0, 1),
            (error, 0, 4),
            (basis, 0, 1),
            (own_v, 0, 1),
            (other_v, 0, 1),
        ],
        [((tokens, width), bf16, 0, 4), ((n_y * n_z, n_t, rank, lanes), WIRE, 0, 4)],
        scalar=where,
    )
    terms = terms.reshape(n_y * n_z, n_t * rank, lanes)
    terms, activ_late, normed_late = lax.optimization_barrier((terms, activ_own, normed_own))
    terms = exchange(terms, ("y", "z"))
    section_grad = call(
        section_kernel,
        [
            (activ_late, 0, 1),
            (norm_gain, 0, 1),
            (upstream, 0, 1),
            (up_other, 0, 1),
            (weights, 0, steps),
            (weights_other, 0, steps),
        ],
        [((tokens, width), bf16, 0, 4)],
        scratch=[pltpu.VMEM((tokens, width), f32)],
        scalar=where,
    )
    own = call(
        own_kernel,
        [(normed_late, 1, 4), (upstream, 0, 1), (error, 0, 4)],
        [((width, 2 * columns), bf16, 0, 4)],
        scalar=where,
    )
    received = lax.ppermute(section_grad, "pipe", [(1, 0)])
    terms, activ_other, own = lax.optimization_barrier((terms, activ_other, own))
    terms = added(terms).reshape(1, n_t, rank, lanes)
    terms = jnp.broadcast_to(terms, (n_x, n_t, rank, lanes)).reshape(n_x * n_t, rank, lanes)
    summed = added(exchange(terms, ("xh", "tensor")))
    summed, own = lax.optimization_barrier((summed, own))
    summed = exchange(jnp.broadcast_to(summed[None], (n_y * n_z,) + summed.shape), ("y", "z"))
    merged = call(
        merged_kernel,
        [
            (activ_other, 0, 4),
            (norm_gain, 0, 1),
            (upstream, 0, 1),
            (own, 0, 4),
        ],
        [((width, 2 * columns), bf16, 0, 4)],
        scratch=[pltpu.VMEM((tokens, 1), f32)],
        scalar=where,
    )
    summed, merged, received = lax.optimization_barrier((summed, merged, received))
    near = n_y * n_x
    right_terms, gram = call(
        right_kernel,
        [(summed, 0, 4), (merged, 0, 4)],
        [((near, rank, columns), f32, 0, 1), ((rank, rank), f32, 0, 1)],
    )
    right_terms = exchange(right_terms, ("y", "xh"))
    left, left_parts, inverse = call(
        left_kernel,
        [(gram, 0, 1), (summed, 0, 4)],
        [
            ((rank, width), f32, 1, 4),
            ((width, 4 * rank), bf16, 0, 4),
            ((rank, rank), f32, 0, 1),
        ],
        scratch=[pltpu.VMEM((rank, rank), f32)],
    )
    right_terms, left, left_parts, inverse, received = lax.optimization_barrier(
        (right_terms, left, left_parts, inverse, received)
    )
    last = lax.axis_index("pipe") == n_p - 1
    received = jnp.where(last, jnp.zeros_like(received), received)
    right_terms = jnp.broadcast_to(right_terms.sum(0)[None], (n_z, rank, columns))
    right_terms = exchange(right_terms, "z")
    right_terms, received = lax.optimization_barrier((right_terms, received))
    mean_right, right_parts, squares = call(
        functools.partial(mean_kernel, replicas=replicas),
        [(right_terms, 0, 1), (inverse, 0, 1)],
        [
            ((rank, columns), f32, 0, 1),
            ((4 * rank, columns), bf16, 0, 1),
            ((rank, columns), f32, 0, 1),
        ],
        limit=8 * 1024 * 1024,
    )
    total = (
        squares
        + lax.ppermute(squares, "pipe", SWAP)
        + lax.ppermute(squares, "tensor", SWAP)
        + lax.ppermute(squares, ("pipe", "tensor"), [(0, 3), (3, 0), (1, 2), (2, 1)])
    )
    error_next = call(
        error_kernel,
        [
            (merged, 0, 4),
            (left_parts, 0, 4),
            (right_parts, 0, 1),
        ],
        [((width, columns), bf16, 0, 4)],
    )
    entries = mean_right.size * n_p * n_t
    factor = jnp.minimum(1.0, clip_level * math.sqrt(entries) / jnp.sqrt(total + 1e-06))
    return (
        received[None],
        left.T[None],
        (mean_right * factor).T[None],
        error_next[None],
    )


def solution(mesh):
    inner = Mesh(
        mesh.devices.reshape((8, 4, 2, mesh.shape["pipe"], mesh.shape["tensor"])),
        DP + ("pipe", "tensor"),
    )
    return jax.shard_map(
        local,
        mesh=inner,
        in_specs=(
            P("pipe", DP + ("tensor",), None),
            P("pipe", None),
            P("pipe", None, "tensor"),
            P("pipe", DP, "tensor"),
            P("pipe", DP, "tensor"),
            P("pipe", "tensor", None),
        ),
        out_specs=(
            P("pipe", DP + ("tensor",), None),
            P("pipe", "tensor", None),
            P("pipe", "tensor", None),
            P("pipe", DP, "tensor"),
        ),
        check_vma=False,
    )
```

```python
import functools
import math

import jax
import jax.numpy as jnp
from jax import lax
from jax.experimental import pallas as pl
from jax.experimental.pallas import tpu as pltpu
from jax.sharding import Mesh, PartitionSpec as P

epsilon = 1e-05
clip_level = 0.25
DP = ("z", "y", "xh")
f32 = jnp.float32
bf16 = jnp.bfloat16
WIRE = f32
SWAP = [(0, 1), (1, 0)]
LIMIT = 60 * 1024 * 1024


def dot(left, right, left_dim, right_dim, precision=None):
    return lax.dot_general(
        left,
        right,
        (((left_dim,), (right_dim,)), ((), ())),
        precision=precision,
        preferred_element_type=f32,
    )


def exact(left, right, left_dim, right_dim):
    return dot(left, right, left_dim, right_dim, lax.Precision.HIGHEST)


def pieces(value, count):
    found = []
    for _ in range(count - 1):
        part = value.astype(bf16)
        found.append(part)
        value = value - part.astype(f32)
    found.append(value.astype(bf16))
    return found


def exchange(chunks, axis):
    return lax.all_to_all(chunks, axis, 0, 0, tiled=False)


def added(terms):
    return terms.astype(f32).sum(0).astype(terms.dtype)


class Stream:
    def __init__(self, far, near, done, dim, parts, begin=0):
        self.far, self.near, self.done, self.dim, self.parts = far, near, done, dim, parts
        self.size = near.shape[dim] // parts
        self.begin = begin
        self.waited = set()

    def place(self, part, begin=0):
        return (slice(None),) * self.dim + (pl.ds(begin + part * self.size, self.size),)

    def bring(self, part):
        source = self.far.at[self.place(part, self.begin)]
        return pltpu.make_async_copy(source, self.near.at[self.place(part)], self.done.at[part])

    def send(self, part):
        place = self.place(part)
        return pltpu.make_async_copy(self.near.at[place], self.far.at[place], self.done.at[part])

    def __call__(self, part=0):
        if part not in self.waited:
            self.bring(part).wait()
            self.waited.add(part)
        return self.near.at[self.place(part)]

    def all(self):
        for part in range(self.parts):
            self(part)
        return self.near

    def out(self, part=0):
        return self.near.at[self.place(part)]


def call(kernel, ins, outs, scratch=(), scalar=None, limit=LIMIT):
    n_in, n_out = len(ins), len(outs)
    scalars = [] if scalar is None else [scalar]

    def body(*refs):
        refs = list(refs)
        front = [refs.pop(0)[0] for _ in scalars]
        far, refs = refs[: n_in + n_out], refs[n_in + n_out :]
        own, refs = refs[: len(scratch)], refs[len(scratch) :]
        near, done = refs[: n_in + n_out], refs[n_in + n_out :]
        marks = [item[1:4] for item in ins]
        marks += [(dim, parts) for _, _, dim, parts in outs]
        streams = [Stream(*item, *mark) for *item, mark in zip(far, near, done, marks)]
        sources, targets = streams[:n_in], streams[n_in:]
        for part in range(max(source.parts for source in sources)):
            for source in sources:
                if part < source.parts:
                    source.bring(part).start()
        kernel(*front, *sources, *targets, *own)
        for source in sources:
            source.all()
        for target in targets:
            for part in range(target.parts):
                target.send(part).wait()

    shapes = []
    for array, dim, parts, *cut in ins:
        shape = list(array.shape)
        if cut:
            shape[dim] = cut[1]
        shapes.append((tuple(shape), array.dtype, parts))
    shapes += [(shape, dtype, parts) for shape, dtype, _, parts in outs]
    found = pl.pallas_call(
        body,
        out_shape=tuple(jax.ShapeDtypeStruct(shape, dtype) for shape, dtype, _, _ in outs),
        in_specs=[pl.BlockSpec(memory_space=pltpu.SMEM) for _ in scalars]
        + [pl.BlockSpec(memory_space=pl.ANY) for _ in ins],
        out_specs=tuple(pl.BlockSpec(memory_space=pl.ANY) for _ in outs),
        scratch_shapes=list(scratch)
        + [pltpu.VMEM(shape, dtype) for shape, dtype, _ in shapes]
        + [pltpu.SemaphoreType.DMA((parts,)) for _, _, parts in shapes],
        compiler_params=pltpu.CompilerParams(vmem_limit_bytes=limit),
        cost_estimate=pl.CostEstimate(flops=0, bytes_accessed=0, transcendentals=0),
    )(*scalars, *[item[0] for item in ins])
    return found if n_out > 1 else found[0]


def normed_of(rows, inverse, gain):
    return (rows * inverse * gain).astype(bf16)


def inverse_of(rows):
    return lax.rsqrt(jnp.mean(rows * rows, axis=-1, keepdims=True) + epsilon)


def half(shard, size):
    return pl.ds(pl.multiple_of(shard * size, size), size)


def projected_kernel(shard, upstream, basis, own_out, give_out, rows_out):
    rank, tokens = own_out.near.shape
    upstream()
    rows_out.near = upstream.near.at[half(1 - shard, tokens)]
    rows_out.send(0).start()
    parts = jnp.concatenate(pieces(basis()[...], 2), axis=0)
    for out, side in ((give_out, 1 - shard), (own_out, shard)):
        both = dot(parts, upstream()[half(side, tokens), :], 1, 1)
        out.out()[...] = both[:rank] + both[rank:]
        out.send(0).start()


def terms_kernel(shard, activ, gain, error, basis, own_v, other_v, normed, out):
    rank = basis.near.shape[0]
    lanes = out.near.shape[-1]
    for part in range(activ.parts):
        rows = activ(part)[...].astype(f32)
        normed.out(part)[...] = normed_of(rows, inverse_of(rows), gain()[...])
        normed.send(part).start()
    pair = jnp.concatenate(pieces(basis()[...], 2), axis=0)
    both = jnp.concatenate([own_v()[...], other_v()[...]], axis=0)
    both = jnp.concatenate(pieces(both, 2), axis=0)
    for part in range(error.parts):
        columns = slice(part * error.size, (part + 1) * error.size)
        product = dot(both, normed.near[:, columns], 1, 0)
        product = product[: 2 * rank] + product[2 * rank :]
        from_error = dot(pair, error(part)[...], 1, 1)
        own = product[:rank] + (from_error[:rank] + from_error[rank:])
        other = product[rank:]
        for chunk in range(out.size):
            columns = slice(chunk * lanes, (chunk + 1) * lanes)
            out.out(part)[chunk, shard] = own[:, columns].astype(out.near.dtype)
            out.out(part)[chunk, 1 - shard] = other[:, columns].astype(out.near.dtype)
        out.send(part).start()


def split_out(out, part, value):
    high, low = pieces(value, 2)
    columns = value.shape[1]
    out.out(part)[:, :columns] = high
    out.out(part)[:, columns:] = low
    out.send(part).start()


def joined(both):
    columns = both.shape[1] // 2
    return both[:, :columns].astype(f32) + both[:, columns:].astype(f32)


def own_kernel(shard, normed, upstream, error, out):
    rows = upstream()[half(shard, normed.near.shape[0]), :]
    for part in range(out.parts):
        split_out(out, part, dot(normed(part)[...], rows, 0, 0) + error(part)[...].astype(f32))


def merged_kernel(shard, activ, gain, upstream, own, out, inverse):
    rows = upstream()[half(1 - shard, activ.near.shape[0]), :]
    for part in range(activ.parts):
        place = pl.ds(part * activ.size, activ.size)
        inverse[place, :] = inverse_of(activ(part)[...].astype(f32))
    for part in range(out.parts):
        lanes = slice(part * out.size, (part + 1) * out.size)
        other = normed_of(activ.near[:, lanes].astype(f32), inverse[...], gain()[:, lanes])
        split_out(out, part, dot(other, rows, 0, 0) + joined(own(part)[...]))


def right_kernel(summed, merged, right_out, gram_out):
    rank = summed.near.shape[1]
    columns = merged.near.shape[1] // 2
    gram = right = 0.0
    for part in range(summed.parts):
        chunk = summed(part)
        whole = jnp.concatenate([chunk[i].astype(f32) for i in range(summed.size)], axis=1)
        parts = jnp.concatenate(pieces(whole, 3), axis=0)
        gram = gram + dot(parts, parts, 1, 1)
        right = right + dot(parts, merged(part)[...], 1, 0)
    right = right[:, :columns] + right[:, columns:]
    right = right[:rank] + right[rank : 2 * rank] + right[2 * rank :]
    right_out.out()[...] = jnp.broadcast_to(right[None], right_out.near.shape)
    right_out.send(0).start()
    gram = gram[:rank] + gram[rank : 2 * rank] + gram[2 * rank :]
    gram_out.out()[...] = gram[:, :rank] + gram[:, rank : 2 * rank] + gram[:, 2 * rank :]
    gram_out.send(0).start()


def left_kernel(gram, summed, left_out, parts_out, inverse_out, inverse):
    rank = gram.near.shape[0]
    row = lax.broadcasted_iota(jnp.int32, (rank, rank), 0)
    column = lax.broadcasted_iota(jnp.int32, (rank, rank), 1)
    both = jnp.concatenate([gram()[...], jnp.where(row == column, 1.0, 0.0)], axis=1)
    below = lax.broadcasted_iota(jnp.int32, (rank, 1), 0)
    for k in range(rank):
        scale = lax.rsqrt(both[k : k + 1, k : k + 1])
        pivot = both[k : k + 1, :] * scale
        inverse[k : k + 1, :] = pivot[:, rank:]
        factor = jnp.where(below > k, both[:, k : k + 1] * scale, 0.0)
        both = both - factor * pivot
    inverse_out.out()[...] = inverse[...]
    inverse_out.send(0).start()
    lanes = summed.near.shape[2] * summed.size
    for part in range(summed.parts):
        chunk = summed(part)
        whole = jnp.concatenate([chunk[i].astype(f32) for i in range(summed.size)], axis=1)
        left = exact(inverse[...], whole, 1, 0)
        left_out.out(part)[...] = left
        left_out.send(part).start()
        high, low = pieces(left, 2)
        parts_out.out(part)[...] = jnp.concatenate([high, low, high, high], axis=0).T
        parts_out.send(part).start()


def mean_kernel(terms, inverse, mean_out, parts_out, squares_out, *, replicas):
    total = jnp.sum(terms()[...], axis=0)
    mean = exact(inverse()[...], total, 1, 0) * (1.0 / replicas)
    squares = jnp.sum(jnp.sum(mean * mean, axis=1, keepdims=True), axis=0, keepdims=True)
    squares_out.out()[...] = jnp.broadcast_to(squares, squares_out.near.shape)
    squares_out.send(0).start()
    high, low = pieces(mean, 2)
    parts_out.out()[...] = jnp.concatenate([high, high, low, jnp.zeros_like(low)], axis=0)
    parts_out.send(0).start()
    mean_out.out()[...] = mean
    mean_out.send(0).start()


def error_kernel(merged, left, right, out):
    few = 128
    for part in range(out.parts):
        for start in range(0, out.size, few):
            rows = slice(start, start + few)
            approx = dot(left(part)[rows, :], right()[...], 1, 0)
            out.out(part)[rows, :] = (joined(merged(part)[rows, :]) - approx).astype(bf16)
        out.send(part).start()


def section_kernel(shard, activ, gain, upstream, other, weights, beside, *refs):
    out, scaled = refs
    tokens, width = activ.near.shape
    own = upstream()[half(shard, tokens), :]
    squares = along = 0.0
    for part in range(weights.parts):
        lanes = slice(part * weights.size, (part + 1) * weights.size)
        rows = activ()[:, lanes].astype(f32)
        product = dot(own, weights(part)[...], 1, 1) + dot(other()[...], beside(part)[...], 1, 1)
        product = product * gain()[:, lanes]
        scaled[:, lanes] = product
        squares = squares + jnp.sum(rows * rows, axis=-1, keepdims=True)
        along = along + jnp.sum(rows * product, axis=-1, keepdims=True)
    inverse = lax.rsqrt(squares * (1.0 / width) + epsilon)
    along = along * (1.0 / width) * inverse * inverse * inverse
    few = tokens // out.parts
    for part in range(out.parts):
        rows = slice(part * few, (part + 1) * few)
        value = inverse[rows] * scaled[rows, :] - activ()[rows, :].astype(f32) * along[rows]
        out.out(part)[...] = value.astype(bf16)
        out.send(part).start()


def local(activations, norm_gain, value_weight, upstream_grad, error_buffer, prior_basis):
    activ_own = activations[0]
    weights = value_weight[0]
    upstream = upstream_grad[0]
    error = error_buffer[0]
    basis = prior_basis[0].T
    tokens, width = activ_own.shape
    replica_tokens, columns = upstream.shape
    rank = basis.shape[0]
    shard = lax.axis_index("tensor")
    where = shard.astype(jnp.int32).reshape(1)
    n_y, n_z, n_x = lax.axis_size("y"), lax.axis_size("z"), lax.axis_size("xh")
    n_t, n_p = lax.axis_size("tensor"), lax.axis_size("pipe")
    replicas = n_y * n_z * n_x
    lanes = width // (n_z * n_y)
    steps = 8

    own_v, give_v, up_give = call(
        projected_kernel,
        [(upstream, 0, 1), (basis, 0, 1)],
        [((rank, tokens), f32, 0, 1)] * 2 + [((tokens, columns), bf16, 0, 1)],
        scalar=where,
    )
    other_v = lax.ppermute(give_v, "tensor", SWAP)
    up_other = lax.ppermute(up_give, ("pipe", "tensor"), [(2, 3), (3, 2)])

    other_v, up_other, activ_late, weights_late = lax.optimization_barrier(
        (other_v, up_other, activ_own, weights)
    )
    activ_other = lax.ppermute(activ_late, "tensor", SWAP)
    beside = [(2, 7), (7, 2), (3, 6), (6, 3)]
    weights_other = lax.ppermute(weights_late, ("xh", "pipe", "tensor"), beside)
    normed_own, terms = call(
        terms_kernel,
        [
            (activ_late, 0, 4),
            (norm_gain, 0, 1),
            (error, 0, 4),
            (basis, 0, 1),
            (own_v, 0, 1),
            (other_v, 0, 1),
        ],
        [((tokens, width), bf16, 0, 4), ((n_y * n_z, n_t, rank, lanes), WIRE, 0, 4)],
        scalar=where,
    )
    terms = terms.reshape(n_y * n_z, n_t * rank, lanes)
    terms, activ_late, normed_late = lax.optimization_barrier((terms, activ_own, normed_own))
    terms = exchange(terms, ("y", "z"))
    section_grad = call(
        section_kernel,
        [
            (activ_late, 0, 1),
            (norm_gain, 0, 1),
            (upstream, 0, 1),
            (up_other, 0, 1),
            (weights, 0, steps),
            (weights_other, 0, steps),
        ],
        [((tokens, width), bf16, 0, 4)],
        scratch=[pltpu.VMEM((tokens, width), f32)],
        scalar=where,
    )
    own = call(
        own_kernel,
        [(normed_late, 1, 4), (upstream, 0, 1), (error, 0, 4)],
        [((width, 2 * columns), bf16, 0, 4)],
        scalar=where,
    )
    received = lax.ppermute(section_grad, "pipe", [(1, 0)])
    terms, own = lax.optimization_barrier((terms, own))
    terms = added(terms).reshape(1, n_t, rank, lanes)
    terms = jnp.broadcast_to(terms, (n_x, n_t, rank, lanes)).reshape(n_x * n_t, rank, lanes)
    summed = added(exchange(terms, ("xh", "tensor")))
    summed, own, activ_other = lax.optimization_barrier((summed, own, activ_other))
    summed = exchange(jnp.broadcast_to(summed[None], (n_y * n_z,) + summed.shape), ("y", "z"))
    merged = call(
        merged_kernel,
        [
            (activ_other, 0, 4),
            (norm_gain, 0, 1),
            (upstream, 0, 1),
            (own, 0, 4),
        ],
        [((width, 2 * columns), bf16, 0, 4)],
        scratch=[pltpu.VMEM((tokens, 1), f32)],
        scalar=where,
    )
    summed, merged, received = lax.optimization_barrier((summed, merged, received))
    near = n_y * n_x
    right_terms, gram = call(
        right_kernel,
        [(summed, 0, 4), (merged, 0, 4)],
        [((near, rank, columns), f32, 0, 1), ((rank, rank), f32, 0, 1)],
    )
    right_terms = exchange(right_terms, ("y", "xh"))
    left, left_parts, inverse = call(
        left_kernel,
        [(gram, 0, 1), (summed, 0, 4)],
        [
            ((rank, width), f32, 1, 4),
            ((width, 4 * rank), bf16, 0, 4),
            ((rank, rank), f32, 0, 1),
        ],
        scratch=[pltpu.VMEM((rank, rank), f32)],
    )
    right_terms, left, left_parts, inverse, received = lax.optimization_barrier(
        (right_terms, left, left_parts, inverse, received)
    )
    last = lax.axis_index("pipe") == n_p - 1
    received = jnp.where(last, jnp.zeros_like(received), received)
    right_terms = jnp.broadcast_to(right_terms.sum(0)[None], (n_z, rank, columns))
    right_terms = exchange(right_terms, "z")
    right_terms, received = lax.optimization_barrier((right_terms, received))
    mean_right, right_parts, squares = call(
        functools.partial(mean_kernel, replicas=replicas),
        [(right_terms, 0, 1), (inverse, 0, 1)],
        [
            ((rank, columns), f32, 0, 1),
            ((4 * rank, columns), bf16, 0, 1),
            ((rank, columns), f32, 0, 1),
        ],
        limit=8 * 1024 * 1024,
    )
    total = (
        squares
        + lax.ppermute(squares, "pipe", SWAP)
        + lax.ppermute(squares, "tensor", SWAP)
        + lax.ppermute(squares, ("pipe", "tensor"), [(0, 3), (3, 0), (1, 2), (2, 1)])
    )
    error_next = call(
        error_kernel,
        [
            (merged, 0, 4),
            (left_parts, 0, 4),
            (right_parts, 0, 1),
        ],
        [((width, columns), bf16, 0, 4)],
    )
    entries = mean_right.size * n_p * n_t
    factor = jnp.minimum(1.0, clip_level * math.sqrt(entries) / jnp.sqrt(total + 1e-06))
    return (
        received[None],
        left.T[None],
        (mean_right * factor).T[None],
        error_next[None],
    )


def solution(mesh):
    inner = Mesh(
        mesh.devices.reshape((8, 4, 2, mesh.shape["pipe"], mesh.shape["tensor"])),
        DP + ("pipe", "tensor"),
    )
    return jax.shard_map(
        local,
        mesh=inner,
        in_specs=(
            P("pipe", DP + ("tensor",), None),
            P("pipe", None),
            P("pipe", None, "tensor"),
            P("pipe", DP, "tensor"),
            P("pipe", DP, "tensor"),
            P("pipe", "tensor", None),
        ),
        out_specs=(
            P("pipe", DP + ("tensor",), None),
            P("pipe", "tensor", None),
            P("pipe", "tensor", None),
            P("pipe", DP, "tensor"),
        ),
        check_vma=False,
    )
```
